32 devices in a mesh: draw: 8 (over z, x), vocab: 4 (over y, core).
Axes of the slice: x: 2, y: 2, z: 4, core: 2. Of those that a mesh axis runs over, the one named last changes fastest.
Arguments:
- hidden: bfloat16 [16, 384, 896], P('draw'), may hold values from -256 to 256
- unembed: bfloat16 [896, 76032], P('draw', 'vocab'), may hold values from -1 to 1
- targets: int32 [384], replicated, may hold values from 0 to 76031
Outputs:
- influence: float32 [256, 128], P('draw')
The draws below stay inside these ranges and needn't reach their ends.
All inputs are finite; a program needn't handle non-finite values.
Results may differ from the reference program's by a relative error of at most 0.0003.
Values may be sent and summed in bfloat16 or wider, within the bound.
A program may use at most 192 MiB of HBM per device.

```python
import jax
import jax.numpy as jnp
from jax import lax

D = 896
V = 76032
TRAIN = 256
QUERY = 128
DRAWS = 16
TOK = 384


def pick_slots(key):
    slot_key = jax.random.fold_in(key, 101)
    key_first = jax.random.fold_in(slot_key, 0)
    key_one = jax.random.fold_in(slot_key, 2)
    key_two = jax.random.fold_in(slot_key, 3)
    key_three = jax.random.fold_in(slot_key, 4)
    first_column = jax.random.randint(key_first, (), 0, V)
    token_one = jax.random.randint(key_one, (), 0, TRAIN // 2)
    token_two = jax.random.randint(key_two, (), TRAIN // 2, TRAIN)
    token_three = jax.random.randint(key_three, (), TRAIN, TRAIN + QUERY)
    return (first_column, jnp.stack([token_one, token_two, token_three]))


def base_weight(key):
    values_drawn = jax.random.normal(jax.random.fold_in(key, 202), (D, V), jnp.float32)
    return jnp.clip(values_drawn, -6.0, 6.0) * D ** (-0.5)


def draw_unembed(key, part):
    matrix = base_weight(key)
    return matrix.astype(jnp.bfloat16)


def draw_hidden(key, part):
    hidden_key = jax.random.fold_in(key, 303)
    values_drawn = jnp.clip(jax.random.normal(hidden_key, (DRAWS, TOK, D), jnp.float32), -6.0, 6.0) * 3.0
    return values_drawn.astype(jnp.bfloat16)


def draw_targets(key, part):
    first_column, slot_tokens = pick_slots(key)
    target_ids = jax.random.randint(jax.random.fold_in(key, 404), (TOK,), 0, V)
    marked = jnp.any(jnp.arange(TOK)[:, None] == slot_tokens[None, :], axis=1)
    return jnp.where(marked, first_column, target_ids).astype(jnp.int32)


def setup_inputs(seed: int = 0) -> dict:
    key_of = jax.random.split(jax.random.key(seed), 4)
    return {
        "hidden": draw_hidden(jax.random.fold_in(key_of[3], 71), 0),
        "unembed": draw_unembed(jax.random.fold_in(key_of[3], 71), 0),
        "targets": draw_targets(jax.random.fold_in(key_of[3], 71), 0),
    }


def token_losses(token_rows, unembed, targets):
    logits = jnp.dot(token_rows, unembed, preferred_element_type=jnp.float32)
    row_max = jnp.max(logits, axis=1)
    row_total = jnp.sum(jnp.exp(logits - row_max[:, None]), axis=1)
    chosen = jnp.take_along_axis(logits, targets[:, None].astype(jnp.int32), axis=1)[:, 0]
    return row_max + jnp.log(row_total) - chosen


def covariance(train_losses, query_losses):
    train_centered = train_losses - jnp.mean(train_losses, axis=0, keepdims=True)
    query_centered = query_losses - jnp.mean(query_losses, axis=0, keepdims=True)
    draw_count = train_losses.shape[0]
    return jnp.dot(train_centered.T, query_centered, precision=lax.Precision.HIGHEST, preferred_element_type=jnp.float32) / (draw_count - 1.0)


def reference(hidden, unembed, targets):
    losses = lax.map(lambda token_rows: token_losses(token_rows, unembed, targets), hidden)
    return covariance(losses[:, :TRAIN], losses[:, TRAIN:])
```

```python
import functools

import jax
import jax.numpy as jnp
from jax import lax
from jax.experimental import pallas as pl
from jax.experimental.pallas import tpu as pltpu
from jax.sharding import PartitionSpec as P

MESH = pl.DeviceIdType.MESH
LANES = 128
GROUP = 32
LOWEST = -1e30
WIDEST = 5
NARROW = 2

TRAIN = 256


def swapped(x, axis, stride):
    return lax.ppermute(x, axis, [(i, i ^ 1 << stride) for i in range(lax.axis_size(axis))])


def merged(part, axis, combine):
    gathered = jax.tree.map(lambda a: lax.all_gather(a, axis), part)

    def take(source):
        return jax.tree.map(lambda a: lax.dynamic_index_in_dim(a, source, 0, False), gathered)

    return lax.fori_loop(
        1, lax.axis_size(axis), lambda source, state: combine(state, take(source)), take(0)
    )


def stats_of(logits, targets, first_column):
    row_max = jnp.max(logits, axis=1)
    row_total = jnp.sum(jnp.exp(logits - row_max[:, None]), axis=1)
    indices = first_column + lax.broadcasted_iota(jnp.int32, logits.shape, 1)
    chosen = jnp.sum(jnp.where(indices == targets[:, None], logits, 0.0), axis=1)
    return (row_max, row_total, chosen)


def combine_stats(left_stats, right_stats):
    joined = jnp.maximum(left_stats[0], right_stats[0])
    summed = left_stats[1] * jnp.exp(left_stats[0] - joined) + right_stats[1] * jnp.exp(
        right_stats[0] - joined
    )
    return (joined, summed, left_stats[2] + right_stats[2])


def covariance(train_losses, query_losses):
    train_centered = train_losses - jnp.mean(train_losses, axis=0, keepdims=True)
    query_centered = query_losses - jnp.mean(query_losses, axis=0, keepdims=True)
    draw_count = train_losses.shape[0]
    return jnp.dot(
        train_centered.T,
        query_centered,
        precision=lax.Precision.HIGHEST,
        preferred_element_type=jnp.float32,
    ) / (draw_count - 1.0)


def body(hidden, unembed, targets):
    per_device, tokens_each, model_width = hidden.shape
    draw_devices = lax.axis_size("draw")
    owned_count = TRAIN // draw_devices
    draw_index = lax.axis_index("draw")
    inner_index = draw_index % 4
    column_count = unembed.shape[1]
    quarter_count = column_count // 4
    repeated = jnp.tile(unembed, (1, draw_devices // 4))
    columns = lax.all_to_all(repeated, "draw", split_axis=1, concat_axis=0, tiled=True)
    first_column = lax.axis_index("vocab") * column_count + inner_index * quarter_count
    group_rows = hidden
    for bit_number in (0, 1):
        partner = swapped(group_rows, "draw", bit_number)
        lower_first = jnp.concatenate([group_rows, partner], axis=0)
        upper_first = jnp.concatenate([partner, group_rows], axis=0)
        group_rows = jnp.where(draw_index // 2**bit_number % 2 == 0, lower_first, upper_first)
    group_draws = group_rows.shape[0]
    logits = jnp.dot(
        group_rows.reshape(group_draws * tokens_each, model_width),
        columns,
        preferred_element_type=jnp.float32,
    )
    fresh_stats = stats_of(logits, jnp.tile(targets, group_draws), first_column)
    total_draws = per_device * draw_devices
    group_start = draw_index // 4 * group_draws
    blank_max = jnp.full((total_draws, tokens_each), -1e30, jnp.float32)
    blank_zero = jnp.zeros((total_draws, tokens_each), jnp.float32)
    local_stats = tuple(
        (
            lax.dynamic_update_slice_in_dim(
                blank_table, fresh.reshape(group_draws, tokens_each), group_start, 0
            )
            for blank_table, fresh in zip((blank_max, blank_zero, blank_zero), fresh_stats)
        )
    )
    row_max, row_total, chosen = merged(local_stats, ("draw", "vocab"), combine_stats)
    losses = row_max + jnp.log(row_total) - chosen
    train_losses = lax.dynamic_slice_in_dim(
        losses[:, :TRAIN], draw_index * owned_count, owned_count, 1
    )
    query_losses = losses[:, TRAIN:]
    return covariance(train_losses, query_losses)


def chunk_plan(column_count, draw_devices):
    full_tiles, rest = divmod(column_count, LANES)
    tiles = full_tiles + (rest > 0)
    share = -(-tiles // draw_devices)
    last_full = full_tiles - (draw_devices - 1) * share
    last_count = column_count - (draw_devices - 1) * share * LANES
    return share, last_full, last_count, rest


def cut(start, total, widest):
    pieces = []
    while total:
        width = min(widest, total)
        pieces.append((start * LANES, width * LANES))
        start, total = start + width, total - width
    return pieces


def kernel(
    plan,
    chunks,
    h_ref,
    u_ref,
    tail_ref,
    t_ref,
    out_ref,
    hbuf,
    w,
    wt,
    xbuf,
    mst,
    sst,
    cst,
    stat_out,
    stat_in,
    vocab_out,
    vocab_in,
    loss_out,
    loss_in,
    own_sem,
    hsend,
    hrecv,
    usend,
    urecv,
    ssend,
    srecv,
    vsend,
    vrecv,
    lsend,
    lrecv,
):
    nd, nv = lax.axis_size("draw"), lax.axis_size("vocab")
    share, last_full, last_count, rest = plan
    length = nd // 2
    k, v = lax.axis_index("draw"), lax.axis_index("vocab")
    line, side, core = k // 2, k % 2, v % 2
    depth = u_ref.shape[0]
    block = share * LANES
    full_end = last_full * LANES
    is_last = k == nd - 1
    wide = t_ref.shape[1]

    def draw_peer(j):
        return lax.rem(k + j, nd)

    def vocab_peer(j):
        return lax.rem(v + j, nv)

    def rows_of(source):
        return pl.ds(pl.multiple_of(source * depth, 16), depth)

    barrier = pltpu.get_barrier_semaphore()

    @pl.loop(1, nd)
    def _(j):
        pl.semaphore_signal(barrier, inc=1, device_id=(draw_peer(j), v), device_id_type=MESH)

    @pl.loop(1, nv)
    def _(j):
        pl.semaphore_signal(barrier, inc=1, device_id=(k, vocab_peer(j)), device_id_type=MESH)

    pl.semaphore_wait(barrier, nd + nv - 2)

    def hidden_copy(source, where, own=False):
        slot = 2 * source + core
        target = [
            (jnp.minimum(k + 2, nd - 1), v),
            (jnp.maximum(k - 2, 0), v),
            (k + 1 - 2 * side, v),
            (k, v + 1 - 2 * core),
        ][where]
        return pltpu.make_async_remote_copy(
            src_ref=h_ref.at[core] if own else hbuf.at[slot],
            dst_ref=hbuf.at[slot],
            send_sem=hsend.at[source, where],
            recv_sem=hrecv.at[slot],
            device_id=target,
            device_id_type=MESH,
        )

    def hidden_wait(slot):
        pltpu.make_async_copy(h_ref.at[0], hbuf.at[slot], hrecv.at[slot]).wait()

    can_up, can_down = line + 1 < length, line > 0

    @pl.when(can_up)
    def _():
        hidden_copy(k, 0, own=True).start()

    @pl.when(can_down)
    def _():
        hidden_copy(k, 1, own=True).start()

    hidden_copy(k, 2, own=True).start()
    own_hidden = [
        pltpu.make_async_copy(h_ref.at[i], hbuf.at[2 * k + i], own_sem.at[i]) for i in range(2)
    ]
    for copy in own_hidden:
        copy.start()

    def pieces_of(chunk, last):
        start, width = chunks[chunk]
        if not last or start + width <= full_end:
            return [(u_ref, None, start, width)]
        return [(tail_ref, 0, start, LANES)] if rest and start == full_end else []

    def columns_copy(chunk, target, piece):
        ref, fixed, start, width = piece
        first = pl.multiple_of(target * block + start, LANES) if fixed is None else fixed
        return ref.at[:, pl.ds(first, width)], w.at[rows_of(k), pl.ds(start, width)]

    def for_target(chunk, target, act):
        @pl.when(target < nd - 1)
        def _():
            for piece in pieces_of(chunk, False):
                act(piece)

        @pl.when(target == nd - 1)
        def _():
            for piece in pieces_of(chunk, True):
                act(piece)

    def remote_columns(chunk, target, piece):
        source_ref, target_ref = columns_copy(chunk, target, piece)
        return pltpu.make_async_remote_copy(
            src_ref=source_ref,
            dst_ref=target_ref,
            send_sem=usend.at[chunk, target],
            recv_sem=urecv.at[chunk, k],
            device_id=(target, v),
            device_id_type=MESH,
        )

    def local_columns(chunk, piece):
        source_ref, target_ref = columns_copy(chunk, k, piece)
        return pltpu.make_async_copy(source_ref, target_ref, urecv.at[chunk, k])

    for chunk in range(len(chunks)):

        @pl.loop(1, nd)
        def _(j):
            target = draw_peer(j)
            for_target(chunk, target, lambda piece: remote_columns(chunk, target, piece).start())

        for_target(chunk, k, lambda piece: local_columns(chunk, piece).start())

    def across(source):
        hidden_wait(2 * source + core)
        hidden_copy(source, 3).start()

    across(k + 1 - 2 * side)

    @pl.loop(1, length)
    def _(step):
        @pl.when(line - step >= 0)
        def _():
            source = k - 2 * step
            hidden_wait(2 * source + core)

            @pl.when(can_up)
            def _():
                hidden_copy(source, 0).start()

            hidden_copy(source, 2).start()
            hidden_copy(source, 3).start()

        @pl.when(line + step < length)
        def _():
            source = k + 2 * step
            hidden_wait(2 * source + core)

            @pl.when(can_down)
            def _():
                hidden_copy(source, 1).start()

            hidden_copy(source, 2).start()
            hidden_copy(source, 3).start()

        @pl.when(line - step >= 0)
        def _():
            across(k - 2 * step + 1 - 2 * side)

        @pl.when(line + step < length)
        def _():
            across(k + 2 * step + 1 - 2 * side)

    for copy in own_hidden:
        copy.wait()

    @pl.loop(1, nd)
    def _(j):
        hidden_wait(2 * draw_peer(j) + 1 - core)

    mst[...] = jnp.full_like(mst, LOWEST)
    sst[...] = jnp.zeros_like(sst)
    cst[...] = jnp.zeros_like(cst)

    limit = jnp.where(is_last, last_count, block)
    first_column = v * u_ref.shape[1] + k * block
    relative = t_ref[...] - first_column
    relative = jnp.where((relative >= 0) & (relative < limit), relative, -block)
    relative = jnp.broadcast_to(relative, (8, wide)) - lax.broadcasted_iota(
        jnp.int32, (8, wide), 0
    )

    for chunk, (start, width) in enumerate(chunks):

        @pl.loop(0, nd)
        def _(j):
            source = draw_peer(j)

            def arrived(piece):
                _, _, first, count = piece
                target_ref = w.at[rows_of(source), pl.ds(first, count)]
                pltpu.make_async_copy(
                    u_ref.at[:, pl.ds(0, count)], target_ref, urecv.at[chunk, source]
                ).wait()

            for_target(chunk, k, arrived)

        groups = jnp.clip(limit - start, 0, width) // GROUP
        wt[0:width, :] = w[:, start : start + width].T

        @pl.loop(0, nd)
        def _(pair):
            rows = hbuf[pl.ds(2 * pair, 2)].reshape(wide, hbuf.shape[2])
            xbuf[0:width, :] = lax.dot_general(
                wt[0:width, :], rows, (((1,), (1,)), ((), ())), preferred_element_type=jnp.float32
            )
            old = mst[pair]

            def largest(group, found):
                for r in range(GROUP // 8):
                    at = pl.multiple_of(group * GROUP + r * 8, 8)
                    found = jnp.maximum(found, xbuf[pl.ds(at, 8), :])
                return found

            new = lax.fori_loop(0, groups, largest, old)

            def totals(group, state):
                total, chosen = state
                for r in range(GROUP // 8):
                    at = pl.multiple_of(group * GROUP + r * 8, 8)
                    x = xbuf[pl.ds(at, 8), :]
                    total = total + jnp.exp(x - new)
                    chosen = chosen + jnp.where(relative == start + at, x, 0.0)
                return total, chosen

            total, chosen = lax.fori_loop(
                0, groups, totals, (sst[pair] * jnp.exp(old - new), cst[pair])
            )
            mst[pair] = new
            sst[pair] = total
            cst[pair] = chosen

    @pl.loop(0, nd)
    def _(pair):
        old = mst[pair]
        top = jnp.max(old, axis=0, keepdims=True)
        stat_out[pair] = jnp.zeros(stat_out.shape[1:], jnp.float32)
        stat_out[pair, 0:1, :] = top
        stat_out[pair, 1:2, :] = jnp.sum(sst[pair] * jnp.exp(old - top), axis=0, keepdims=True)
        stat_out[pair, 2:3, :] = jnp.sum(cst[pair], axis=0, keepdims=True)

    def stat_copy(target):
        return pltpu.make_async_remote_copy(
            src_ref=stat_out.at[target],
            dst_ref=stat_in.at[k],
            send_sem=ssend.at[target],
            recv_sem=srecv.at[k],
            device_id=(target, v),
            device_id_type=MESH,
        )

    @pl.loop(1, nd)
    def _(j):
        stat_copy(draw_peer(j)).start()

    def joined(state, part):
        top = jnp.maximum(state[0], part[0:1])
        total = state[1] * jnp.exp(state[0] - top) + part[1:2] * jnp.exp(part[0:1] - top)
        return top, total, state[2] + part[2:3]

    mine = stat_out[k]

    def take_draw(j, state):
        source = draw_peer(j)
        pltpu.make_async_copy(stat_out.at[0], stat_in.at[source], srecv.at[source]).wait()
        return joined(state, stat_in[source])

    state = lax.fori_loop(1, nd, take_draw, (mine[0:1], mine[1:2], mine[2:3]))
    vocab_out[...] = jnp.zeros_like(vocab_out)
    for i in range(3):
        vocab_out[i : i + 1, :] = state[i]

    def vocab_copy(target):
        return pltpu.make_async_remote_copy(
            src_ref=vocab_out,
            dst_ref=vocab_in.at[v],
            send_sem=vsend.at[target],
            recv_sem=vrecv.at[v],
            device_id=(k, target),
            device_id_type=MESH,
        )

    @pl.loop(1, nv)
    def _(j):
        vocab_copy(vocab_peer(j)).start()

    vocab_in[v] = vocab_out[...]

    @pl.loop(1, nv)
    def _(j):
        source = vocab_peer(j)
        pltpu.make_async_copy(vocab_out, vocab_in.at[source], vrecv.at[source]).wait()

    def take_vocab(source, state):
        return joined(state, vocab_in[source])

    first = vocab_in[0]
    top, total, chosen = lax.fori_loop(1, nv, take_vocab, (first[0:1], first[1:2], first[2:3]))
    loss_out[...] = jnp.broadcast_to(top + jnp.log(total) - chosen, loss_out.shape)

    def loss_copy(target):
        return pltpu.make_async_remote_copy(
            src_ref=loss_out,
            dst_ref=loss_in.at[k],
            send_sem=lsend.at[target],
            recv_sem=lrecv.at[k],
            device_id=(target, v),
            device_id_type=MESH,
        )

    @pl.loop(1, nd)
    def _(j):
        loss_copy(draw_peer(j)).start()

    loss_in[k] = loss_out[...]

    @pl.loop(1, nd)
    def _(j):
        source = draw_peer(j)
        pltpu.make_async_copy(loss_out, loss_in.at[source], lrecv.at[source]).wait()

    for source in range(nd):
        out_ref[source : source + 1, :] = loss_in[source, 0:1, :]

    @pl.loop(1, nd)
    def _(j):
        target = draw_peer(j)
        for chunk in range(len(chunks)):
            for_target(
                chunk, target, lambda piece: remote_columns(chunk, target, piece).wait_send()
            )
        stat_copy(target).wait_send()
        loss_copy(target).wait_send()
        hidden_copy(target, 3).wait_send()

    @pl.loop(1, nv)
    def _(j):
        vocab_copy(vocab_peer(j)).wait_send()

    @pl.loop(0, length)
    def _(place):
        source = 2 * place + side

        @pl.when((place <= line) & can_up)
        def _():
            hidden_copy(source, 0).wait_send()

        @pl.when((place >= line) & can_down)
        def _():
            hidden_copy(source, 1).wait_send()

        hidden_copy(source, 2).wait_send()


def fused(plan, hidden, unembed, targets):
    per_device, tokens_each, model_width = hidden.shape
    nd, nv = lax.axis_size("draw"), lax.axis_size("vocab")
    depth, column_count = unembed.shape
    share, last_full, _, rest = plan
    chunks = cut(0, last_full, WIDEST) + cut(last_full, share - last_full, NARROW)
    widest = max(width for _, width in chunks)
    count = len(chunks)
    wide = 2 * tokens_each
    tail = jnp.pad(unembed[:, column_count - rest :], ((0, 0), (0, LANES - rest)))
    f32, bf16, dma = jnp.float32, jnp.bfloat16, pltpu.SemaphoreType.DMA
    anywhere = pl.BlockSpec(memory_space=pl.ANY)
    inside = pl.BlockSpec(memory_space=pltpu.VMEM)
    losses = pl.pallas_call(
        functools.partial(kernel, plan, chunks),
        out_shape=jax.ShapeDtypeStruct((nd, wide), f32),
        in_specs=[anywhere, anywhere, anywhere, inside],
        out_specs=inside,
        scratch_shapes=[
            pltpu.VMEM((2 * nd, tokens_each, model_width), bf16),
            pltpu.VMEM((model_width, share * LANES), bf16),
            pltpu.VMEM((widest, model_width), bf16),
            pltpu.VMEM((widest, wide), f32),
            pltpu.VMEM((nd, 8, wide), f32),
            pltpu.VMEM((nd, 8, wide), f32),
            pltpu.VMEM((nd, 8, wide), f32),
            pltpu.VMEM((nd, 8, wide), f32),
            pltpu.VMEM((nd, 8, wide), f32),
            pltpu.VMEM((8, wide), f32),
            pltpu.VMEM((nv, 8, wide), f32),
            pltpu.VMEM((8, wide), f32),
            pltpu.VMEM((nd, 8, wide), f32),
            dma((2,)),
            dma((nd, 4)),
            dma((2 * nd,)),
            dma((count, nd)),
            dma((count, nd)),
            dma((nd,)),
            dma((nd,)),
            dma((nv,)),
            dma((nv,)),
            dma((nd,)),
            dma((nd,)),
        ],
        compiler_params=pltpu.CompilerParams(
            collective_id=0, has_side_effects=True, vmem_limit_bytes=48 * 1024 * 1024
        ),
    )(hidden, unembed, tail, jnp.tile(targets, 2)[None, :])
    losses = losses.reshape(2 * nd, tokens_each)
    owned_count = TRAIN // nd
    train_losses = lax.dynamic_slice_in_dim(
        losses[:, :TRAIN], lax.axis_index("draw") * owned_count, owned_count, 1
    )
    return covariance(train_losses, losses[:, TRAIN:])


def placed_body(hidden, unembed, targets):
    per_device, tokens_each, model_width = hidden.shape
    nd, nv = lax.axis_size("draw"), lax.axis_size("vocab")
    depth, column_count = unembed.shape
    plan = chunk_plan(column_count, nd)
    share, last_full, last_count, rest = plan
    fits = (
        per_device == 2
        and nd % 2 == 0
        and nv % 2 == 0
        and depth % 16 == 0
        and tokens_each % LANES == 0
        and rest > 0
        and rest % GROUP == 0
        and 0 < last_full < share
        and nd * 2 * tokens_each * model_width * 2 < 16 * 1024 * 1024
    )
    if fits:
        return fused(plan, hidden, unembed, targets)
    return body(hidden, unembed, targets)


def solution(mesh):
    placed = (P("draw", None, None), P("draw", "vocab"), P())
    return jax.shard_map(
        placed_body, mesh=mesh, in_specs=placed, out_specs=P("draw", None), check_vma=False
    )
```

```python
import functools

import jax
import jax.numpy as jnp
from jax import lax
from jax.experimental import pallas as pl
from jax.experimental.pallas import tpu as pltpu
from jax.sharding import PartitionSpec as P

MESH = pl.DeviceIdType.MESH
LANES = 128
GROUP = 32
LOWEST = -1e30
WIDEST = 5
NARROW = 2
FINE = 2
FINE_CHUNKS = 2
SEND_COUNTS = (1, 1, 1, 2, 2, 2)

TRAIN = 256


def swapped(x, axis, stride):
    return lax.ppermute(x, axis, [(i, i ^ 1 << stride) for i in range(lax.axis_size(axis))])


def merged(part, axis, combine):
    gathered = jax.tree.map(lambda a: lax.all_gather(a, axis), part)

    def take(source):
        return jax.tree.map(lambda a: lax.dynamic_index_in_dim(a, source, 0, False), gathered)

    return lax.fori_loop(
        1, lax.axis_size(axis), lambda source, state: combine(state, take(source)), take(0)
    )


def stats_of(logits, targets, first_column):
    row_max = jnp.max(logits, axis=1)
    row_total = jnp.sum(jnp.exp(logits - row_max[:, None]), axis=1)
    indices = first_column + lax.broadcasted_iota(jnp.int32, logits.shape, 1)
    chosen = jnp.sum(jnp.where(indices == targets[:, None], logits, 0.0), axis=1)
    return (row_max, row_total, chosen)


def combine_stats(left_stats, right_stats):
    joined = jnp.maximum(left_stats[0], right_stats[0])
    summed = left_stats[1] * jnp.exp(left_stats[0] - joined) + right_stats[1] * jnp.exp(
        right_stats[0] - joined
    )
    return (joined, summed, left_stats[2] + right_stats[2])


def covariance(train_losses, query_losses):
    train_centered = train_losses - jnp.mean(train_losses, axis=0, keepdims=True)
    query_centered = query_losses - jnp.mean(query_losses, axis=0, keepdims=True)
    draw_count = train_losses.shape[0]
    return jnp.dot(
        train_centered.T,
        query_centered,
        precision=lax.Precision.HIGHEST,
        preferred_element_type=jnp.float32,
    ) / (draw_count - 1.0)


def body(hidden, unembed, targets):
    per_device, tokens_each, model_width = hidden.shape
    draw_devices = lax.axis_size("draw")
    owned_count = TRAIN // draw_devices
    draw_index = lax.axis_index("draw")
    inner_index = draw_index % 4
    column_count = unembed.shape[1]
    quarter_count = column_count // 4
    repeated = jnp.tile(unembed, (1, draw_devices // 4))
    columns = lax.all_to_all(repeated, "draw", split_axis=1, concat_axis=0, tiled=True)
    first_column = lax.axis_index("vocab") * column_count + inner_index * quarter_count
    group_rows = hidden
    for bit_number in (0, 1):
        partner = swapped(group_rows, "draw", bit_number)
        lower_first = jnp.concatenate([group_rows, partner], axis=0)
        upper_first = jnp.concatenate([partner, group_rows], axis=0)
        group_rows = jnp.where(draw_index // 2**bit_number % 2 == 0, lower_first, upper_first)
    group_draws = group_rows.shape[0]
    logits = jnp.dot(
        group_rows.reshape(group_draws * tokens_each, model_width),
        columns,
        preferred_element_type=jnp.float32,
    )
    fresh_stats = stats_of(logits, jnp.tile(targets, group_draws), first_column)
    total_draws = per_device * draw_devices
    group_start = draw_index // 4 * group_draws
    blank_max = jnp.full((total_draws, tokens_each), -1e30, jnp.float32)
    blank_zero = jnp.zeros((total_draws, tokens_each), jnp.float32)
    local_stats = tuple(
        (
            lax.dynamic_update_slice_in_dim(
                blank_table, fresh.reshape(group_draws, tokens_each), group_start, 0
            )
            for blank_table, fresh in zip((blank_max, blank_zero, blank_zero), fresh_stats)
        )
    )
    row_max, row_total, chosen = merged(local_stats, ("draw", "vocab"), combine_stats)
    losses = row_max + jnp.log(row_total) - chosen
    train_losses = lax.dynamic_slice_in_dim(
        losses[:, :TRAIN], draw_index * owned_count, owned_count, 1
    )
    query_losses = losses[:, TRAIN:]
    return covariance(train_losses, query_losses)


def chunk_plan(column_count, draw_devices):
    full_tiles, rest = divmod(column_count, LANES)
    tiles = full_tiles + (rest > 0)
    share = -(-tiles // draw_devices)
    last_full = full_tiles - (draw_devices - 1) * share
    last_count = column_count - (draw_devices - 1) * share * LANES
    return share, last_full, last_count, rest


def cut(start, total, widest):
    pieces = []
    while total:
        width = min(widest, total)
        pieces.append((start * LANES, width * LANES))
        start, total = start + width, total - width
    return pieces


def unrolled(first, last, step, state):
    for i in range(first, last):
        state = step(i, state)
    return state


def kernel(
    plan,
    chunks,
    sends,
    h_ref,
    u_ref,
    tail_ref,
    t_ref,
    out_ref,
    hbuf,
    w,
    wt,
    xbuf,
    xbuf_other,
    mst,
    sst,
    cst,
    stat_out,
    stat_in,
    vocab_out,
    vocab_in,
    loss_out,
    loss_in,
    own_sem,
    hsend,
    hrecv,
    usend,
    urecv,
    ssend,
    srecv,
    vsend,
    vrecv,
    lsend,
    lrecv,
):
    nd, nv = lax.axis_size("draw"), lax.axis_size("vocab")
    share, last_full, last_count, rest = plan
    length = nd // 2
    k, v = lax.axis_index("draw"), lax.axis_index("vocab")
    line, side, core = k // 2, k % 2, v % 2
    depth = u_ref.shape[0]
    block = share * LANES
    full_end = last_full * LANES
    is_last = k == nd - 1
    wide = t_ref.shape[1]

    def draw_peer(j):
        return lax.rem(k + j, nd)

    def vocab_peer(j):
        return lax.rem(v + j, nv)

    def rows_of(source):
        return pl.ds(pl.multiple_of(source * depth, 16), depth)

    barrier = pltpu.get_barrier_semaphore()

    @pl.loop(1, nd)
    def _(j):
        pl.semaphore_signal(barrier, inc=1, device_id=(draw_peer(j), v), device_id_type=MESH)

    @pl.loop(1, nv)
    def _(j):
        pl.semaphore_signal(barrier, inc=1, device_id=(k, vocab_peer(j)), device_id_type=MESH)

    pl.semaphore_wait(barrier, nd + nv - 2)

    half = h_ref.shape[1] // 2

    def part_of(ref, index, part):
        return ref.at[index, pl.ds(pl.multiple_of(part // 2 * half, 16), half)]

    def hidden_copy(source, where, own=False):
        beside = v + 2 - 4 * (v // 2)
        part = beside if where == 5 else v
        place = part_of(hbuf, 2 * source + part % 2, part)
        target = [
            (jnp.minimum(k + 2, nd - 1), v),
            (jnp.maximum(k - 2, 0), v),
            (k + 1 - 2 * side, v),
            (k, beside),
            (k, v + 1 - 2 * core),
            (k, v + 1 - 2 * core),
        ][where]
        return pltpu.make_async_remote_copy(
            src_ref=part_of(h_ref, part % 2, part) if own else place,
            dst_ref=place,
            send_sem=hsend.at[source, where],
            recv_sem=hrecv.at[source, part],
            device_id=target,
            device_id_type=MESH,
        )

    def hidden_wait(source, part):
        pltpu.make_async_copy(
            part_of(h_ref, 0, part),
            part_of(hbuf, 2 * source + part % 2, part),
            hrecv.at[source, part],
        ).wait()

    can_up, can_down = line + 1 < length, line > 0

    @pl.when(can_up)
    def _():
        hidden_copy(k, 0, own=True).start()

    @pl.when(can_down)
    def _():
        hidden_copy(k, 1, own=True).start()

    hidden_copy(k, 2, own=True).start()
    own_hidden = [
        pltpu.make_async_copy(h_ref.at[i], hbuf.at[2 * k + i], own_sem.at[i]) for i in range(2)
    ]
    for copy in own_hidden:
        copy.start()

    def pieces_of(chunk, last):
        start, width = sends[chunk]
        if not last or start + width <= full_end:
            return [(u_ref, None, start, width)]
        return [(tail_ref, 0, start, LANES)] if rest and start == full_end else []

    def columns_copy(chunk, target, piece):
        ref, fixed, start, width = piece
        first = pl.multiple_of(target * block + start, LANES) if fixed is None else fixed
        return ref.at[:, pl.ds(first, width)], w.at[rows_of(k), pl.ds(start, width)]

    def for_target(chunk, target, act):
        @pl.when(target < nd - 1)
        def _():
            for piece in pieces_of(chunk, False):
                act(piece)

        @pl.when(target == nd - 1)
        def _():
            for piece in pieces_of(chunk, True):
                act(piece)

    def remote_columns(chunk, target, piece):
        source_ref, target_ref = columns_copy(chunk, target, piece)
        return pltpu.make_async_remote_copy(
            src_ref=source_ref,
            dst_ref=target_ref,
            send_sem=usend.at[chunk, target],
            recv_sem=urecv.at[chunk, k],
            device_id=(target, v),
            device_id_type=MESH,
        )

    def local_columns(chunk, piece):
        source_ref, target_ref = columns_copy(chunk, k, piece)
        return pltpu.make_async_copy(source_ref, target_ref, urecv.at[chunk, k])

    def send_columns(chunk):
        @pl.loop(1, nd)
        def _(j):
            target = draw_peer(j)
            for_target(chunk, target, lambda piece: remote_columns(chunk, target, piece).start())

        for_target(chunk, k, lambda piece: local_columns(chunk, piece).start())

    def at_distance(step, act):
        if step == 0:
            act(k, None)
        elif 0 < step < length:

            @pl.when(line - step >= 0)
            def _():
                act(k - 2 * step, (can_up, 0))

            @pl.when(line + step < length)
            def _():
                act(k + 2 * step, (can_down, 1))

    def along(source, onward):
        if onward is not None:
            hidden_wait(source, v)
            more, where = onward

            @pl.when(more)
            def _():
                hidden_copy(source, where).start()

            for where in (2, 3, 4):
                hidden_copy(source, where).start()

    def across(source, onward):
        source = source + 1 - 2 * side
        hidden_wait(source, v)
        for where in (3, 4):
            hidden_copy(source, where).start()

    def beside_along(source, onward):
        if onward is not None:
            hidden_wait(source, v + 2 - 4 * (v // 2))
            hidden_copy(source, 5).start()

    def beside_across(source, onward):
        source = source + 1 - 2 * side
        hidden_wait(source, v + 2 - 4 * (v // 2))
        hidden_copy(source, 5).start()

    sent = 0
    for step in range(length + 2):
        at_distance(step, along)
        at_distance(step - 1, across)
        at_distance(step - 1, beside_along)
        at_distance(step - 2, beside_across)
        count = SEND_COUNTS[step] if step < len(SEND_COUNTS) else 0
        for chunk in range(sent, min(sent + count, len(sends))):
            send_columns(chunk)
        sent = min(sent + count, len(sends))
    for chunk in range(sent, len(sends)):
        send_columns(chunk)

    for copy in own_hidden:
        copy.wait()

    @pl.loop(1, nd)
    def _(j):
        for part in range(2):
            hidden_wait(draw_peer(j), 2 * part + 1 - core)

    mst[...] = jnp.full_like(mst, LOWEST)
    sst[...] = jnp.zeros_like(sst)
    cst[...] = jnp.zeros_like(cst)

    limit = jnp.where(is_last, last_count, block)
    first_column = v * u_ref.shape[1] + k * block
    relative = t_ref[...] - first_column
    relative = jnp.where((relative >= 0) & (relative < limit), relative, -block)
    relative = jnp.broadcast_to(relative, (8, wide)) - lax.broadcasted_iota(
        jnp.int32, (8, wide), 0
    )

    for chunk, (start, width) in enumerate(chunks):

        @pl.loop(0, nd)
        def _(j):
            source = draw_peer(j)

            for part, (first, count) in enumerate(sends):
                if start <= first < start + width:

                    def arrived(piece):
                        target_ref = w.at[rows_of(source), pl.ds(piece[2], piece[3])]
                        pltpu.make_async_copy(
                            u_ref.at[:, pl.ds(0, piece[3])], target_ref, urecv.at[part, source]
                        ).wait()

                    for_target(part, k, arrived)

        wt[0:width, :] = w[:, start : start + width].T

        def multiply(pair, x_ref):
            rows = hbuf[pl.ds(2 * pair, 2)].reshape(wide, hbuf.shape[2])
            x_ref[0:width, :] = lax.dot_general(
                wt[0:width, :], rows, (((1,), (1,)), ((), ())), preferred_element_type=jnp.float32
            )

        def gather(pair, x_ref):
            if start + width <= full_end:
                loop, groups = unrolled, width // GROUP
            else:
                loop, groups = lax.fori_loop, jnp.clip(limit - start, 0, width) // GROUP
            old = mst[pair]

            def largest(group, found):
                for r in range(GROUP // 8):
                    at = group * GROUP + r * 8
                    found = jnp.maximum(found, x_ref[pl.ds(at, 8), :])
                return found

            new = loop(0, groups, largest, old)

            def totals(group, state):
                total, chosen = state
                for r in range(GROUP // 8):
                    at = group * GROUP + r * 8
                    x = x_ref[pl.ds(at, 8), :]
                    total = total + jnp.exp(x - new)
                    chosen = jnp.where(relative == start + at, x, chosen)
                return total, chosen

            total, chosen = loop(
                0, groups, totals, (sst[pair] * jnp.exp(old - new), cst[pair])
            )
            mst[pair] = new
            sst[pair] = total
            cst[pair] = chosen

        multiply(0, xbuf)

        @pl.loop(0, nd // 2)
        def _(i):
            multiply(2 * i + 1, xbuf_other)
            gather(2 * i, xbuf)
            multiply(jnp.minimum(2 * i + 2, nd - 1), xbuf)
            gather(2 * i + 1, xbuf_other)

    @pl.loop(0, nd)
    def _(pair):
        old = mst[pair]
        top = jnp.max(old, axis=0, keepdims=True)
        stat_out[pair] = jnp.zeros(stat_out.shape[1:], jnp.float32)
        stat_out[pair, 0:1, :] = top
        stat_out[pair, 1:2, :] = jnp.sum(sst[pair] * jnp.exp(old - top), axis=0, keepdims=True)
        stat_out[pair, 2:3, :] = jnp.sum(cst[pair], axis=0, keepdims=True)

    def stat_copy(target):
        return pltpu.make_async_remote_copy(
            src_ref=stat_out.at[target],
            dst_ref=stat_in.at[k],
            send_sem=ssend.at[target],
            recv_sem=srecv.at[k],
            device_id=(target, v),
            device_id_type=MESH,
        )

    @pl.loop(1, nd)
    def _(j):
        stat_copy(draw_peer(j)).start()

    def joined(state, part):
        top = jnp.maximum(state[0], part[0:1])
        total = state[1] * jnp.exp(state[0] - top) + part[1:2] * jnp.exp(part[0:1] - top)
        return top, total, state[2] + part[2:3]

    mine = stat_out[k]

    def take_draw(j, state):
        source = draw_peer(j)
        pltpu.make_async_copy(stat_out.at[0], stat_in.at[source], srecv.at[source]).wait()
        return joined(state, stat_in[source])

    state = lax.fori_loop(1, nd, take_draw, (mine[0:1], mine[1:2], mine[2:3]))
    vocab_out[...] = jnp.zeros_like(vocab_out)
    for i in range(3):
        vocab_out[i : i + 1, :] = state[i]

    def vocab_copy(target):
        return pltpu.make_async_remote_copy(
            src_ref=vocab_out,
            dst_ref=vocab_in.at[v],
            send_sem=vsend.at[target],
            recv_sem=vrecv.at[v],
            device_id=(k, target),
            device_id_type=MESH,
        )

    @pl.loop(1, nv)
    def _(j):
        vocab_copy(vocab_peer(j)).start()

    vocab_in[v] = vocab_out[...]

    @pl.loop(1, nv)
    def _(j):
        source = vocab_peer(j)
        pltpu.make_async_copy(vocab_out, vocab_in.at[source], vrecv.at[source]).wait()

    def take_vocab(source, state):
        return joined(state, vocab_in[source])

    first = vocab_in[0]
    top, total, chosen = lax.fori_loop(1, nv, take_vocab, (first[0:1], first[1:2], first[2:3]))
    loss_out[...] = jnp.broadcast_to(top + jnp.log(total) - chosen, loss_out.shape)

    def loss_copy(target):
        return pltpu.make_async_remote_copy(
            src_ref=loss_out,
            dst_ref=loss_in.at[k],
            send_sem=lsend.at[target],
            recv_sem=lrecv.at[k],
            device_id=(target, v),
            device_id_type=MESH,
        )

    @pl.loop(1, nd)
    def _(j):
        loss_copy(draw_peer(j)).start()

    loss_in[k] = loss_out[...]

    @pl.loop(1, nd)
    def _(j):
        source = draw_peer(j)
        pltpu.make_async_copy(loss_out, loss_in.at[source], lrecv.at[source]).wait()

    for source in range(nd):
        out_ref[source : source + 1, :] = loss_in[source, 0:1, :]

    @pl.loop(1, nd)
    def _(j):
        target = draw_peer(j)
        for chunk in range(len(sends)):
            for_target(
                chunk, target, lambda piece: remote_columns(chunk, target, piece).wait_send()
            )
        stat_copy(target).wait_send()
        loss_copy(target).wait_send()
        for where in (3, 4, 5):
            hidden_copy(target, where).wait_send()

    @pl.loop(1, nv)
    def _(j):
        vocab_copy(vocab_peer(j)).wait_send()

    @pl.loop(0, length)
    def _(place):
        source = 2 * place + side

        @pl.when((place <= line) & can_up)
        def _():
            hidden_copy(source, 0).wait_send()

        @pl.when((place >= line) & can_down)
        def _():
            hidden_copy(source, 1).wait_send()

        hidden_copy(source, 2).wait_send()


def fused(plan, hidden, unembed, targets):
    per_device, tokens_each, model_width = hidden.shape
    nd, nv = lax.axis_size("draw"), lax.axis_size("vocab")
    depth, column_count = unembed.shape
    share, last_full, _, rest = plan
    chunks = cut(0, last_full, WIDEST) + cut(last_full, share - last_full, NARROW)
    sends = []
    for chunk, (start, width) in enumerate(chunks):
        sends += cut(start // LANES, width // LANES, FINE if chunk < FINE_CHUNKS else WIDEST)
    widest = max(width for _, width in chunks)
    count = len(sends)
    wide = 2 * tokens_each
    tail = jnp.pad(unembed[:, column_count - rest :], ((0, 0), (0, LANES - rest)))
    f32, bf16, dma = jnp.float32, jnp.bfloat16, pltpu.SemaphoreType.DMA
    anywhere = pl.BlockSpec(memory_space=pl.ANY)
    inside = pl.BlockSpec(memory_space=pltpu.VMEM)
    losses = pl.pallas_call(
        functools.partial(kernel, plan, chunks, sends),
        out_shape=jax.ShapeDtypeStruct((nd, wide), f32),
        in_specs=[anywhere, anywhere, anywhere, inside],
        out_specs=inside,
        scratch_shapes=[
            pltpu.VMEM((2 * nd, tokens_each, model_width), bf16),
            pltpu.VMEM((model_width, share * LANES), bf16),
            pltpu.VMEM((widest, model_width), bf16),
            pltpu.VMEM((widest, wide), f32),
            pltpu.VMEM((widest, wide), f32),
            pltpu.VMEM((nd, 8, wide), f32),
            pltpu.VMEM((nd, 8, wide), f32),
            pltpu.VMEM((nd, 8, wide), f32),
            pltpu.VMEM((nd, 8, wide), f32),
            pltpu.VMEM((nd, 8, wide), f32),
            pltpu.VMEM((8, wide), f32),
            pltpu.VMEM((nv, 8, wide), f32),
            pltpu.VMEM((8, wide), f32),
            pltpu.VMEM((nd, 8, wide), f32),
            dma((2,)),
            dma((nd, 6)),
            dma((nd, 4)),
            dma((count, nd)),
            dma((count, nd)),
            dma((nd,)),
            dma((nd,)),
            dma((nv,)),
            dma((nv,)),
            dma((nd,)),
            dma((nd,)),
        ],
        compiler_params=pltpu.CompilerParams(
            collective_id=0, has_side_effects=True, vmem_limit_bytes=60 * 1024 * 1024
        ),
    )(hidden, unembed, tail, jnp.tile(targets, 2)[None, :])
    losses = losses.reshape(2 * nd, tokens_each)
    owned_count = TRAIN // nd
    train_losses = lax.dynamic_slice_in_dim(
        losses[:, :TRAIN], lax.axis_index("draw") * owned_count, owned_count, 1
    )
    return covariance(train_losses, losses[:, TRAIN:])


def placed_body(hidden, unembed, targets):
    per_device, tokens_each, model_width = hidden.shape
    nd, nv = lax.axis_size("draw"), lax.axis_size("vocab")
    depth, column_count = unembed.shape
    plan = chunk_plan(column_count, nd)
    share, last_full, last_count, rest = plan
    fits = (
        per_device == 2
        and nd % 2 == 0
        and nv == 4
        and depth % 16 == 0
        and tokens_each % LANES == 0
        and tokens_each % 32 == 0
        and rest > 0
        and rest % GROUP == 0
        and 0 < last_full < share
        and nd * 2 * tokens_each * model_width * 2 < 16 * 1024 * 1024
    )
    if fits:
        return fused(plan, hidden, unembed, targets)
    return body(hidden, unembed, targets)


def solution(mesh):
    placed = (P("draw", None, None), P("draw", "vocab"), P())
    return jax.shard_map(
        placed_body, mesh=mesh, in_specs=placed, out_specs=P("draw", None), check_vma=False
    )
```
